32 devices in a mesh: row: 4 (over z), col: 8 (over y, x, core).
Axes of the slice: x: 2, y: 2, z: 4, core: 2. Of those that a mesh axis runs over, the one named last changes fastest.
Arguments:
- amplitudes: bfloat16 [4, 256, 4096], P('row', 'col'), may hold values from -6 to 6
- integrals: bfloat16 [512, 4096], P('col', 'row'), may hold values from -0.125 to 0.125
- panel_owner: int32 [4, 8], P('row'), may hold values from 0 to 7, each once within a row
- residual_in: float32 [4, 256, 512], P(None, 'col', 'row'), may hold values from -6 to 6
Outputs:
- residual_out: float32 [4, 256, 512], P(None, 'col', 'row')
The draws below stay inside these ranges and needn't reach their ends.
Inputs may be any that keep to these rules, and one draw needn't show every extreme that they name: `panel_owner`: each row is a permutation of 0 to 7.
All inputs are finite; a program needn't handle non-finite values.
Results may differ from the reference program's by a relative error of at most 0.0003.
Values may be sent and summed in bfloat16 or wider, within the bound.
No kernel may reach another device: no remote copies, remote signals or barrier semaphores. Data moves between devices by JAX's collectives and lax.ppermute only.
A program may use at most 64 MiB of HBM per device.

```python
import jax
import jax.numpy as jnp
from jax import lax

PAIR_DEV = 32
K_ROW = 1024
KW = 4096
AB = 512
N_ROW = 4
N_COL = 8


def with_spikes(drawn, stream_key, source, target, blocks, factor):
    def block_of(position):
        return (jnp.arange(drawn.shape[position]) // (drawn.shape[position] // blocks)).reshape((-1,) + (1,) * (drawn.ndim - 1 - position))

    first = jax.random.permutation(stream_key, blocks)[block_of(target)]
    other_side = (block_of(target) + blocks // 2) % blocks
    return jnp.where((block_of(source) == first) | (block_of(source) == other_side), factor * drawn, drawn)


def block_scale(key, extent, split, low, largest):
    factor_of, own = 1.0, jax.random.fold_in(key, 6)
    for position, blocks in split:
        draws = jnp.exp(jax.random.uniform(jax.random.fold_in(own, position), (blocks,), jnp.float32, low / len(split), largest / len(split)))
        factor_of = factor_of * jnp.repeat(draws, extent[position] // blocks).reshape([-1 if axis == position else 1 for axis in range(len(extent))])
    return factor_of


def gaussian(stream_key, dims, spread, reach, shards=(), dtype=jnp.bfloat16):
    result = spread * jax.random.normal(stream_key, dims, jnp.float32)
    if shards:
        result = result * block_scale(stream_key, dims, shards, -0.22, 0.18)
    return jnp.clip(result, -reach, reach).astype(dtype)


def bell_draw_with(rng, dims, deviation, most, shards, heavy, dtype=jnp.bfloat16):
    array = deviation * jax.random.normal(rng, dims, jnp.float32)
    if shards:
        array = array * block_scale(rng, dims, shards, -0.22, 0.18)
    return jnp.clip(with_spikes(array, jax.random.fold_in(rng, 3), *heavy), -most, most).astype(dtype)


def setup_inputs(seed: int = 0) -> dict:
    arg_keys = jax.random.split(jax.random.key(seed), 5)
    amplitudes = gaussian(arg_keys[0], (N_ROW, N_COL * PAIR_DEV, KW), 1.0, 6.0, ((0, 4), (1, 8)))
    integrals = bell_draw_with(arg_keys[1], (AB, KW), KW ** -0.5, 0.125, ((0, 8), (1, 4)), (1, 0, 8, 2.0))
    panel_owner = jax.vmap(lambda own: jax.random.permutation(own, N_COL))(jax.random.split(arg_keys[2], N_ROW)).reshape((N_ROW, N_COL)).astype(jnp.int32)
    residual_in = gaussian(arg_keys[3], (N_ROW, N_COL * PAIR_DEV, AB), 1.0, 6.0, ((1, 8), (2, 4)), jnp.float32)
    return dict(amplitudes=amplitudes, integrals=integrals, panel_owner=panel_owner, residual_in=residual_in)


def reference(amplitudes, integrals, panel_owner, residual_in):
    ab_block = AB // N_COL
    pair_rows = amplitudes.reshape(-1, KW)
    inverse = jnp.argsort(panel_owner, axis=1).astype(jnp.int32)
    stored = integrals.reshape(N_COL, ab_block, KW)
    accumulated = residual_in.reshape(-1, AB).astype(jnp.float32)
    for row_group in range(N_ROW):
        cd_block = stored[:, :, row_group * K_ROW:(row_group + 1) * K_ROW]
        ordered = jnp.take(cd_block, inverse[row_group], axis=0).reshape(AB, K_ROW)
        partial_value = lax.dot_general(pair_rows[:, row_group * K_ROW:(row_group + 1) * K_ROW], ordered,
                                  (((1,), (1,)), ((), ())), preferred_element_type=jnp.float32)
        accumulated = accumulated + partial_value
    return accumulated.reshape(residual_in.shape)
```

```python
import functools
import math

import jax
import jax.numpy as jnp
from jax import lax
from jax.experimental import pallas as pl
from jax.experimental.pallas import tpu as pltpu
from jax.sharding import PartitionSpec as P

VMEM = pl.BlockSpec(memory_space=pltpu.VMEM)
ANY = pl.BlockSpec(memory_space=pl.ANY)
SMEM = pl.BlockSpec(memory_space=pltpu.SMEM)


def exchange(value, axis, step):
    n = lax.axis_size(axis)
    return lax.ppermute(value, axis, [(i, i ^ step) for i in range(n)])


def split_kernel(amp_ref, *outs):
    width = outs[0].shape[-1]
    row = lax.axis_index("row")
    for step, out in enumerate(outs):
        at = pl.multiple_of((row ^ step) * width, width)
        out[...] = amp_ref[0, :, pl.ds(at, width)]


def call(kernel, outs, specs, args, scratch=()):
    held = [*outs, *args, *(s for s in scratch if s.dtype in (jnp.float32, jnp.bfloat16))]
    size = sum(math.prod(x.shape) * jnp.dtype(x.dtype).itemsize for x in held)
    return pl.pallas_call(
        kernel, out_shape=outs, in_specs=specs, out_specs=[VMEM] * len(outs), scratch_shapes=scratch,
        compiler_params=pltpu.CompilerParams(vmem_limit_bytes=size + (2 << 20)),
    )(*args)


def split_amplitudes(amplitudes, rows):
    _, pairs, kw = amplitudes.shape
    block = jax.ShapeDtypeStruct((pairs, kw // rows), amplitudes.dtype)
    return call(split_kernel, [block] * rows, [VMEM], [amplitudes])


def assemble_kernel(steps, *refs):
    rows = len(steps)
    amps, panels, (lhs, near) = refs[:rows], refs[rows:-2], refs[-2:]
    pairs, height = amps[0].shape[0], panels[0].shape[0]
    row = lax.axis_index("row")
    for step, amp in zip(steps, amps):
        at = pl.multiple_of((row ^ step) * pairs, pairs)
        lhs[pl.ds(at, pairs), :] = amp[...]
    for index, panel in enumerate(panels):
        near[index * height:(index + 1) * height, :] = panel[...]


def assemble(steps, amps, panels):
    outs = [jax.ShapeDtypeStruct((len(blocks) * blocks[0].shape[0], blocks[0].shape[1]), blocks[0].dtype)
            for blocks in (amps, panels)]
    args = [*amps, *panels]
    return call(functools.partial(assemble_kernel, steps), outs, [VMEM] * len(args), args)


def contract_kernel(steps, owner_ref, residual_ref, lhs, near, far, *refs):
    outs, (weights, residual, sem) = refs[:len(steps)], refs[len(steps):]
    fetch = pltpu.make_async_copy(residual_ref, residual, sem)
    fetch.start()
    width = outs[0].shape[1]
    row, col = lax.axis_index("row"), lax.axis_index("col")
    columns = owner_ref.shape[1]
    height = weights.shape[0] // columns
    per_row = width // height
    for step in range(columns):
        owner = owner_ref[0, col ^ step]
        place = ((owner // per_row) ^ row) * per_row + owner % per_row
        at = pl.multiple_of(place * height, height)
        held, index = (near, far)[step % 2], step // 2
        weights[pl.ds(at, height), :] = held[index * height:(index + 1) * height, :]
    for step, out in zip(steps, outs):
        part = lax.dot_general(
            lhs[...], weights[step * width:(step + 1) * width, :],
            (((1,), (1,)), ((), ())), preferred_element_type=jnp.float32)
        if step == 0:
            fetch.wait()
            part = part + residual[...].reshape(part.shape)
        out[...] = part


def contract(steps, owner, residual, lhs, near, far):
    rows, ab, depth = len(steps), 2 * near.shape[0], near.shape[1]
    part = jax.ShapeDtypeStruct((lhs.shape[0], ab // rows), jnp.float32)
    return call(
        functools.partial(contract_kernel, steps), [part] * rows, [SMEM, ANY, VMEM, VMEM, VMEM],
        [owner, residual, lhs, near, far],
        [pltpu.VMEM((ab, depth), jnp.bfloat16), pltpu.VMEM(residual.shape, jnp.float32), pltpu.SemaphoreType.DMA],
    )


def shards(amplitudes, integrals, panel_owner, residual_in):
    rows, columns = lax.axis_size("row"), lax.axis_size("col")
    steps = tuple(range(rows - 1, -1, -1))
    panels = [exchange(integrals, "col", step) if step else integrals for step in range(0, columns, 2)]
    blocks = split_amplitudes(amplitudes, rows)
    amps = [exchange(blocks[step], "row", step) if step else blocks[0] for step in steps]
    lhs, near = assemble(steps, amps, panels)
    parts = contract(steps, panel_owner, residual_in, lhs, near, exchange(near, "col", 1))
    total = parts[-1]
    for step, part in zip(steps[:-1], parts):
        total = total + exchange(part, "row", step)
    return total.reshape(residual_in.shape)


def solution(mesh):
    placed = (P("row", "col", None), P("col", "row"), P("row", None), P(None, "col", "row"))
    return jax.shard_map(
        shards, mesh=mesh, in_specs=placed, out_specs=P(None, "col", "row"), check_vma=False
    )
```

```python
import functools
import math

import jax
import jax.numpy as jnp
from jax import lax
from jax.experimental import pallas as pl
from jax.experimental.pallas import tpu as pltpu
from jax.sharding import PartitionSpec as P

VMEM = pl.BlockSpec(memory_space=pltpu.VMEM)
SMEM = pl.BlockSpec(memory_space=pltpu.SMEM)


def exchange(value, axis, step):
    n = lax.axis_size(axis)
    return lax.ppermute(value, axis, [(i, i ^ step) for i in range(n)])


def split_kernel(amp_ref, *outs):
    width = outs[0].shape[-1]
    row = lax.axis_index("row")
    for step, out in enumerate(outs):
        at = pl.multiple_of((row ^ step) * width, width)
        out[...] = amp_ref[0, :, pl.ds(at, width)]


def call(kernel, outs, specs, args, scratch=()):
    held = [*outs, *args, *scratch]
    size = sum(math.prod(x.shape) * jnp.dtype(x.dtype).itemsize for x in held)
    return pl.pallas_call(
        kernel, out_shape=outs, in_specs=specs, out_specs=[VMEM] * len(outs), scratch_shapes=scratch,
        compiler_params=pltpu.CompilerParams(vmem_limit_bytes=size + (2 << 20)),
    )(*args)


def split_amplitudes(amplitudes, rows):
    _, pairs, kw = amplitudes.shape
    block = jax.ShapeDtypeStruct((pairs, kw // rows), amplitudes.dtype)
    return call(split_kernel, [block] * rows, [VMEM], [amplitudes])


def assemble_kernel(steps, residual_ref, *refs):
    rows = len(steps)
    panels, amps, (residual, near, lhs) = refs[:-rows - 3], refs[-rows - 3:-3], refs[-3:]
    pairs, height = amps[0].shape[0], panels[0].shape[0]
    row = lax.axis_index("row")
    for step, amp in zip(steps, amps):
        at = pl.multiple_of((row ^ step) * pairs, pairs)
        lhs[pl.ds(at, pairs), :] = amp[...]
    for index, panel in enumerate(panels):
        near[index * height:(index + 1) * height, :] = panel[...]
    residual[...] = residual_ref[...]


def assemble(steps, residual, panels, amps):
    outs = [jax.ShapeDtypeStruct((len(blocks) * blocks[0].shape[0], blocks[0].shape[1]), blocks[0].dtype)
            for blocks in (panels, amps)]
    outs = [jax.ShapeDtypeStruct(residual.shape, residual.dtype)] + outs
    args = [residual, *panels, *amps]
    return call(functools.partial(assemble_kernel, steps), outs, [VMEM] * len(args), args)


def contract_kernel(steps, owner_ref, residual_ref, lhs, near, far, *refs):
    outs, weights = refs[:-1], refs[-1]
    width = outs[0].shape[1]
    row, col = lax.axis_index("row"), lax.axis_index("col")
    columns = owner_ref.shape[1]
    height = weights.shape[0] // columns
    per_row = width // height
    for step in range(columns):
        owner = owner_ref[0, col ^ step]
        place = ((owner // per_row) ^ row) * per_row + owner % per_row
        at = pl.multiple_of(place * height, height)
        held, index = (near, far)[step % 2], step // 2
        weights[pl.ds(at, height), :] = held[index * height:(index + 1) * height, :]
    for step, out in zip(steps, outs):
        part = lax.dot_general(
            lhs[...], weights[step * width:(step + 1) * width, :],
            (((1,), (1,)), ((), ())), preferred_element_type=jnp.float32)
        if step == 0:
            part = part + residual_ref[...].reshape(part.shape)
        out[...] = part


def contract(steps, owner, residual, lhs, near, far):
    rows, ab, depth = len(steps), 2 * near.shape[0], near.shape[1]
    part = jax.ShapeDtypeStruct((lhs.shape[0], ab // rows), jnp.float32)
    return call(
        functools.partial(contract_kernel, steps), [part] * rows, [SMEM, VMEM, VMEM, VMEM, VMEM],
        [owner, residual, lhs, near, far],
        [pltpu.VMEM((ab, depth), jnp.bfloat16)],
    )


def shards(amplitudes, integrals, panel_owner, residual_in):
    rows, columns = lax.axis_size("row"), lax.axis_size("col")
    steps = tuple(range(rows - 1, -1, -1))
    panels = [exchange(integrals, "col", step) if step else integrals for step in range(0, columns, 2)]
    blocks = split_amplitudes(amplitudes, rows)
    amps = [exchange(blocks[step], "row", step) if step else blocks[0] for step in steps]
    residual, near, lhs = assemble(steps, residual_in, panels, amps)
    parts = contract(steps, panel_owner, residual, lhs, near, exchange(near, "col", 1))
    total = parts[-1]
    for step, part in zip(steps[:-1], parts):
        total = total + exchange(part, "row", step)
    return total.reshape(residual_in.shape)


def solution(mesh):
    placed = (P("row", "col", None), P("col", "row"), P("row", None), P(None, "col", "row"))
    return jax.shard_map(
        shards, mesh=mesh, in_specs=placed, out_specs=P(None, "col", "row"), check_vma=False
    )
```

```python
import functools
import math

import jax
import jax.numpy as jnp
from jax import lax
from jax.experimental import pallas as pl
from jax.experimental.pallas import tpu as pltpu
from jax.sharding import PartitionSpec as P

VMEM = pl.BlockSpec(memory_space=pltpu.VMEM)
SCALE_ROWS = 16
SMEM = pl.BlockSpec(memory_space=pltpu.SMEM)


def exchange(value, axis, step):
    n = lax.axis_size(axis)
    return lax.ppermute(value, axis, [(i, i ^ step) for i in range(n)])


def split_kernel(panel_ref, amp_ref, own_ref, *outs):
    own_ref[...] = panel_ref[...]
    width = outs[0].shape[-1]
    row = lax.axis_index("row")
    for step, out in enumerate(outs):
        at = pl.multiple_of((row ^ step) * width, width)
        out[...] = amp_ref[0, :, pl.ds(at, width)]


def call(kernel, outs, specs, args, scratch=()):
    held = [*outs, *args, *scratch]
    size = sum(math.prod(x.shape) * jnp.dtype(x.dtype).itemsize for x in held)
    return pl.pallas_call(
        kernel, out_shape=outs, in_specs=specs, out_specs=[VMEM] * len(outs), scratch_shapes=scratch,
        compiler_params=pltpu.CompilerParams(vmem_limit_bytes=size + (2 << 20)),
    )(*args)


def split_amplitudes(integrals, amplitudes, rows):
    _, pairs, kw = amplitudes.shape
    block = jax.ShapeDtypeStruct((pairs, kw // rows), amplitudes.dtype)
    outs = [jax.ShapeDtypeStruct(integrals.shape, integrals.dtype)] + [block] * rows
    own, *blocks = call(split_kernel, outs, [VMEM, VMEM], [integrals, amplitudes])
    return own, blocks


def assemble_kernel(steps, owner_ref, residual_ref, *refs):
    rows = len(steps)
    panels, amps, (owner, residual, near, lhs) = refs[:-rows - 4], refs[-rows - 4:-4], refs[-4:]
    pairs, height = amps[0].shape[0], panels[0].shape[0]
    row = lax.axis_index("row")
    for step, amp in zip(steps, amps):
        at = pl.multiple_of((row ^ step) * pairs, pairs)
        lhs[pl.ds(at, pairs), :] = amp[...]
    for index, panel in enumerate(panels):
        near[index * height:(index + 1) * height, :] = panel[...]
    residual[...] = residual_ref[...]
    owner[...] = owner_ref[...]


def assemble(steps, owner, residual, panels, amps):
    outs = [jax.ShapeDtypeStruct((len(blocks) * blocks[0].shape[0], blocks[0].shape[1]), blocks[0].dtype)
            for blocks in (panels, amps)]
    outs = [jax.ShapeDtypeStruct(x.shape, x.dtype) for x in (owner, residual)] + outs
    args = [owner, residual, *panels, *amps]
    return call(functools.partial(assemble_kernel, steps), outs, [VMEM] * len(args), args)


def contract_kernel(steps, owner_ref, residual_ref, lhs, near, far, *refs):
    outs, weights = refs[:-1], refs[-1]
    width = outs[0].shape[1]
    row, col = lax.axis_index("row"), lax.axis_index("col")
    columns = owner_ref.shape[1]
    height = weights.shape[0] // columns
    per_row = width // height
    for step in range(columns):
        owner = owner_ref[0, col ^ step]
        place = ((owner // per_row) ^ row) * per_row + owner % per_row
        at = pl.multiple_of(place * height, height)
        held, index = (near, far)[step % 2], step // 2
        weights[pl.ds(at, height), :] = held[index * height:(index + 1) * height, :]
    for step, out in zip(steps, outs):
        part = lax.dot_general(
            lhs[...], weights[step * width:(step + 1) * width, :],
            (((1,), (1,)), ((), ())), preferred_element_type=jnp.float32)
        if step == 0:
            out[...] = part + residual_ref[...].reshape(part.shape)
        else:
            largest = jnp.max(jnp.abs(part), axis=0, keepdims=True)
            power = jnp.clip(14.0 - jnp.ceil(jnp.log2(jnp.maximum(largest, 1e-36))), -60.0, 120.0)
            out[:part.shape[0], :] = part * jnp.exp2(power)
            out[part.shape[0]:, :] = jnp.broadcast_to(power, (SCALE_ROWS, part.shape[1]))


def contract(steps, owner, residual, lhs, near, far):
    rows, ab, depth = len(steps), 2 * near.shape[0], near.shape[1]
    outs = [
        jax.ShapeDtypeStruct((lhs.shape[0] + (SCALE_ROWS if step else 0), ab // rows), jnp.float32) for step in steps]
    return call(
        functools.partial(contract_kernel, steps), outs, [SMEM, VMEM, VMEM, VMEM, VMEM],
        [owner, residual, lhs, near, far],
        [pltpu.VMEM((ab, depth), jnp.bfloat16)],
    )


def exchange_partial(part, step):
    got = exchange(part.astype(jnp.float16), "row", step).astype(jnp.float32)
    return got[:-SCALE_ROWS] * jnp.exp2(-got[-SCALE_ROWS:1 - SCALE_ROWS])


def shards(amplitudes, integrals, panel_owner, residual_in):
    rows, columns = lax.axis_size("row"), lax.axis_size("col")
    steps = tuple(range(rows - 1, -1, -1))
    own, blocks = split_amplitudes(integrals, amplitudes, rows)
    panels = [exchange(own, "col", step) if step else own for step in range(0, columns, 2)]
    amps = [exchange(blocks[step], "row", step) if step else blocks[0] for step in steps]
    owner, residual, near, lhs = assemble(steps, panel_owner, residual_in, panels, amps)
    parts = contract(steps, owner, residual, lhs, near, exchange(near, "col", 1))
    total = parts[-1]
    for step, part in zip(steps[:-1], parts):
        total = total + exchange_partial(part, step)
    return total.reshape(residual_in.shape)


def solution(mesh):
    placed = (P("row", "col", None), P("col", "row"), P("row", None), P(None, "col", "row"))
    return jax.shard_map(
        shards, mesh=mesh, in_specs=placed, out_specs=P(None, "col", "row"), check_vma=False
    )
```

```python
import functools
import math

import jax
import jax.numpy as jnp
from jax import lax
from jax.experimental import pallas as pl
from jax.experimental.pallas import tpu as pltpu
from jax.sharding import PartitionSpec as P

VMEM = pl.BlockSpec(memory_space=pltpu.VMEM)
HBM = pl.BlockSpec(memory_space=pltpu.HBM)
SMEM = pl.BlockSpec(memory_space=pltpu.SMEM)


def exchange(value, axis, step):
    n = lax.axis_size(axis)
    return lax.ppermute(value, axis, [(i, i ^ step) for i in range(n)])


def like(array, *shape):
    return jax.ShapeDtypeStruct(shape or array.shape, array.dtype)


def call(kernel, outs, specs, args, scratch=(), semaphores=()):
    size = sum(math.prod(x.shape) * jnp.dtype(x.dtype).itemsize for x in [*outs, *args, *scratch])
    return pl.pallas_call(
        kernel, out_shape=outs, in_specs=specs, out_specs=[VMEM] * len(outs), scratch_shapes=[*scratch, *semaphores],
        compiler_params=pltpu.CompilerParams(vmem_limit_bytes=size + (2 << 20)),
    )(*args)


def fetch_kernel(panel_ref, amp_ref, residual_ref, owner_ref, *refs):
    panel, residual, owner, blocks, sems = refs[0], refs[1], refs[2], refs[3:-1], refs[-1]
    width = blocks[0].shape[-1]
    row = lax.axis_index("row")
    pairs = [(panel_ref, panel), (residual_ref, residual), (owner_ref, owner)]
    for step, block in enumerate(blocks):
        at = pl.multiple_of((row ^ step) * width, width)
        pairs.append((amp_ref.at[0, :, pl.ds(at, width)], block))
    copies = [pltpu.make_async_copy(source, target, sems.at[i]) for i, (source, target) in enumerate(pairs)]
    for copy in copies:
        copy.start()
    for copy in copies:
        copy.wait()


def fetch(integrals, amplitudes, residual, owner, rows):
    _, pairs, kw = amplitudes.shape
    outs = [like(integrals), like(residual), like(owner)] + [like(amplitudes, pairs, kw // rows)] * rows
    args = [integrals, amplitudes, residual, owner]
    panel, residual, owner, *blocks = call(
        fetch_kernel, outs, [HBM] * 4, args, semaphores=[pltpu.SemaphoreType.DMA((len(outs),))])
    return panel, residual, owner, blocks


def assemble_kernel(count, *refs):
    panels, amps, (near, early) = refs[:count], refs[count:-2], refs[-2:]
    for blocks, out in ((panels, near), (amps, early)):
        height = blocks[0].shape[0]
        for index, block in enumerate(blocks):
            out[index * height:(index + 1) * height, :] = block[...]


def assemble(panels, amps):
    outs = [like(blocks[0], len(blocks) * blocks[0].shape[0], blocks[0].shape[1]) for blocks in (panels, amps)]
    args = [*panels, *amps]
    return call(functools.partial(assemble_kernel, len(panels)), outs, [VMEM] * len(args), args)


def contract_kernel(steps, owner_ref, residual_ref, early, late, near, far, *refs):
    outs, (lhs, weights) = refs[:len(steps)], refs[len(steps):]
    width, pairs = outs[0].shape[1], late.shape[0]
    row, col = lax.axis_index("row"), lax.axis_index("col")
    columns = owner_ref.shape[1]
    height = weights.shape[0] // columns
    per_row = width // height
    for index, step in enumerate([step for step in steps if step != 1]):
        at = pl.multiple_of((row ^ step) * pairs, pairs)
        lhs[pl.ds(at, pairs), :] = early[index * pairs:(index + 1) * pairs, :]
    lhs[pl.ds(pl.multiple_of((row ^ 1) * pairs, pairs), pairs), :] = late[...]
    for step in range(columns):
        owner = owner_ref[0, col ^ step]
        place = ((owner // per_row) ^ row) * per_row + owner % per_row
        at = pl.multiple_of(place * height, height)
        held, index = (near, far)[step % 2], step // 2
        weights[pl.ds(at, height), :] = held[index * height:(index + 1) * height, :]
    for step, out in zip(steps, outs):
        part = lax.dot_general(
            lhs[...], weights[step * width:(step + 1) * width, :],
            (((1,), (1,)), ((), ())), preferred_element_type=jnp.float32)
        if step == 0:
            part = part + residual_ref[...].reshape(part.shape)
        out[...] = part


def contract(steps, owner, residual, early, late, near, far):
    rows, ab, depth = len(steps), 2 * near.shape[0], near.shape[1]
    total = early.shape[0] + late.shape[0]
    part = jax.ShapeDtypeStruct((total, ab // rows), jnp.float32)
    return call(
        functools.partial(contract_kernel, steps), [part] * rows, [SMEM] + [VMEM] * 5,
        [owner, residual, early, late, near, far],
        [pltpu.VMEM((total, depth), jnp.bfloat16), pltpu.VMEM((ab, depth), jnp.bfloat16)],
    )


def shards(amplitudes, integrals, panel_owner, residual_in):
    rows, columns = lax.axis_size("row"), lax.axis_size("col")
    steps = tuple(range(rows - 1, -1, -1))
    own, residual, owner, blocks = fetch(integrals, amplitudes, residual_in, panel_owner, rows)
    panels = [exchange(own, "col", step) if step else own for step in range(0, columns, 2)]
    amps = {step: exchange(blocks[step], "row", step) if step else blocks[0] for step in steps}
    near, early = assemble(panels, [amps[step] for step in steps if step != 1])
    parts = contract(steps, owner, residual, early, amps[1], near, exchange(near, "col", 1))
    total = parts[-1]
    for step, part in zip(steps[:-1], parts):
        total = total + exchange(part, "row", step)
    return total.reshape(residual_in.shape)


def solution(mesh):
    placed = (P("row", "col", None), P("col", "row"), P("row", None), P(None, "col", "row"))
    return jax.shard_map(
        shards, mesh=mesh, in_specs=placed, out_specs=P(None, "col", "row"), check_vma=False
    )
```

```python
import functools
import math

import jax
import jax.numpy as jnp
from jax import lax
from jax.experimental import pallas as pl
from jax.experimental.pallas import tpu as pltpu
from jax.sharding import PartitionSpec as P

VMEM = pl.BlockSpec(memory_space=pltpu.VMEM)
HBM = pl.BlockSpec(memory_space=pltpu.HBM)
SMEM = pl.BlockSpec(memory_space=pltpu.SMEM)


def exchange(value, axis, step):
    n = lax.axis_size(axis)
    return lax.ppermute(value, axis, [(i, i ^ step) for i in range(n)])


def like(array, *shape):
    return jax.ShapeDtypeStruct(shape or array.shape, array.dtype)


def call(kernel, outs, specs, args, scratch=(), semaphores=()):
    size = sum(math.prod(x.shape) * jnp.dtype(x.dtype).itemsize for x in [*outs, *args, *scratch])
    return pl.pallas_call(
        kernel, out_shape=outs, in_specs=specs, out_specs=[VMEM] * len(outs), scratch_shapes=[*scratch, *semaphores],
        compiler_params=pltpu.CompilerParams(vmem_limit_bytes=size + (2 << 20)),
    )(*args)


def fetch_kernel(panel_ref, amp_ref, residual_ref, owner_ref, *refs):
    panel, residual, owner, blocks, sems = refs[0], refs[1], refs[2], refs[3:-1], refs[-1]
    width = blocks[0].shape[-1]
    row = lax.axis_index("row")
    pairs = [(panel_ref, panel), (residual_ref, residual), (owner_ref, owner)]
    for step, block in enumerate(blocks):
        at = pl.multiple_of((row ^ step) * width, width)
        pairs.append((amp_ref.at[0, :, pl.ds(at, width)], block))
    copies = [pltpu.make_async_copy(source, target, sems.at[i]) for i, (source, target) in enumerate(pairs)]
    for copy in copies:
        copy.start()
    for copy in copies:
        copy.wait()


def fetch(integrals, amplitudes, residual, owner, rows):
    _, pairs, kw = amplitudes.shape
    outs = [like(integrals), like(residual), like(owner)] + [like(amplitudes, pairs, kw // rows)] * rows
    args = [pltpu.with_memory_space_constraint(x, pltpu.HBM) for x in (integrals, amplitudes, residual, owner)]
    panel, residual, owner, *blocks = call(
        fetch_kernel, outs, [HBM] * 4, args, semaphores=[pltpu.SemaphoreType.DMA((len(outs),))])
    return panel, residual, owner, blocks


def assemble_kernel(steps, *refs):
    rows = len(steps)
    panels, amps, (near, lhs) = refs[:-rows - 2], refs[-rows - 2:-2], refs[-2:]
    height, pairs = panels[0].shape[0], amps[0].shape[0]
    row = lax.axis_index("row")
    for index, panel in enumerate(panels):
        near[index * height:(index + 1) * height, :] = panel[...]
    for step, amp in zip(steps, amps):
        at = pl.multiple_of((row ^ step) * pairs, pairs)
        lhs[pl.ds(at, pairs), :] = amp[...]


def assemble(steps, panels, amps):
    outs = [like(blocks[0], len(blocks) * blocks[0].shape[0], blocks[0].shape[1]) for blocks in (panels, amps)]
    args = [*panels, *amps]
    return call(functools.partial(assemble_kernel, steps), outs, [VMEM] * len(args), args)


def product(panels, lhs):
    return lax.dot_general(panels[...], lhs[...], (((1,), (1,)), ((), ())), preferred_element_type=jnp.float32)


def near_kernel(near, lhs, out):
    out[...] = product(near, lhs)


def contract_near(near, lhs):
    out = jax.ShapeDtypeStruct((near.shape[0], lhs.shape[0]), jnp.float32)
    return call(near_kernel, [out], [VMEM, VMEM], [near, lhs])[0]


def contract_kernel(steps, owner_ref, residual_ref, lhs, near_part, far, *refs):
    outs, ordered = refs[:-1], refs[-1]
    width = outs[0].shape[1]
    row, col = lax.axis_index("row"), lax.axis_index("col")
    columns = owner_ref.shape[1]
    height = ordered.shape[0] // columns
    per_row = width // height
    for half, part in enumerate((near_part[...], product(far, lhs))):
        for index in range(columns // 2):
            owner = owner_ref[0, col ^ (2 * index + half)]
            place = ((owner // per_row) ^ row) * per_row + owner % per_row
            at = pl.multiple_of(place * height, height)
            ordered[pl.ds(at, height), :] = part[index * height:(index + 1) * height, :]
    for step, out in zip(steps, outs):
        part = ordered[step * width:(step + 1) * width, :].T
        if step == 0:
            part = part + residual_ref[...].reshape(part.shape)
        out[...] = part


def contract(steps, owner, residual, lhs, near_part, far):
    rows, ab = len(steps), 2 * far.shape[0]
    part = jax.ShapeDtypeStruct((lhs.shape[0], ab // rows), jnp.float32)
    return call(
        functools.partial(contract_kernel, steps), [part] * rows, [SMEM] + [VMEM] * 4,
        [owner, residual, lhs, near_part, far], [pltpu.VMEM((ab, lhs.shape[0]), jnp.float32)],
    )


def shards(amplitudes, integrals, panel_owner, residual_in):
    rows, columns = lax.axis_size("row"), lax.axis_size("col")
    steps = tuple(range(rows - 1, -1, -1))
    own, residual, owner, blocks = fetch(integrals, amplitudes, residual_in, panel_owner, rows)
    panels = [exchange(own, "col", step) if step else own for step in range(0, columns, 2)]
    amps = [exchange(blocks[step], "row", step) if step else blocks[0] for step in steps]
    near, lhs = assemble(steps, panels, amps)
    far = exchange(near, "col", 1)
    parts = contract(steps, owner, residual, lhs, contract_near(near, lhs), far)
    total = parts[-1]
    for step, part in zip(steps[:-1], parts):
        total = total + exchange(part, "row", step)
    return total.reshape(residual_in.shape)


def solution(mesh):
    placed = (P("row", "col", None), P("col", "row"), P("row", None), P(None, "col", "row"))
    return jax.shard_map(
        shards, mesh=mesh, in_specs=placed, out_specs=P(None, "col", "row"), check_vma=False
    )
```

```python
import functools
import math

import jax
import jax.numpy as jnp
from jax import lax
from jax.experimental import pallas as pl
from jax.experimental.pallas import tpu as pltpu
from jax.sharding import PartitionSpec as P

VMEM = pl.BlockSpec(memory_space=pltpu.VMEM)
HBM = pl.BlockSpec(memory_space=pltpu.HBM)
SCALE_ROWS = 16
SMEM = pl.BlockSpec(memory_space=pltpu.SMEM)


def exchange(value, axis, step):
    n = lax.axis_size(axis)
    return lax.ppermute(value, axis, [(i, i ^ step) for i in range(n)])


def like(array, *shape):
    return jax.ShapeDtypeStruct(shape or array.shape, array.dtype)


def call(kernel, outs, specs, args, scratch=(), semaphores=()):
    size = sum(math.prod(x.shape) * jnp.dtype(x.dtype).itemsize for x in [*outs, *args, *scratch])
    return pl.pallas_call(
        kernel, out_shape=outs, in_specs=specs, out_specs=[VMEM] * len(outs), scratch_shapes=[*scratch, *semaphores],
        compiler_params=pltpu.CompilerParams(vmem_limit_bytes=size + (2 << 20)),
    )(*args)


def fetch_kernel(panel_ref, amp_ref, residual_ref, owner_ref, *refs):
    panel, residual, owner, blocks, sems = refs[0], refs[1], refs[2], refs[3:-1], refs[-1]
    width = blocks[0].shape[-1]
    row = lax.axis_index("row")
    pairs = [(panel_ref, panel), (residual_ref, residual), (owner_ref, owner)]
    for step, block in enumerate(blocks):
        at = pl.multiple_of((row ^ step) * width, width)
        pairs.append((amp_ref.at[0, :, pl.ds(at, width)], block))
    copies = [pltpu.make_async_copy(source, target, sems.at[i]) for i, (source, target) in enumerate(pairs)]
    for copy in copies:
        copy.start()
    for copy in copies:
        copy.wait()


def fetch(integrals, amplitudes, residual, owner, rows):
    _, pairs, kw = amplitudes.shape
    outs = [like(integrals), like(residual), like(owner)] + [like(amplitudes, pairs, kw // rows)] * rows
    args = [pltpu.with_memory_space_constraint(x, pltpu.HBM) for x in (integrals, amplitudes, residual, owner)]
    panel, residual, owner, *blocks = call(
        fetch_kernel, outs, [HBM] * 4, args, semaphores=[pltpu.SemaphoreType.DMA((len(outs),))])
    return panel, residual, owner, blocks


def assemble_kernel(steps, *refs):
    rows = len(steps)
    panels, amps, (near, lhs) = refs[:-rows - 2], refs[-rows - 2:-2], refs[-2:]
    height, pairs = panels[0].shape[0], amps[0].shape[0]
    row = lax.axis_index("row")
    for index, panel in enumerate(panels):
        near[index * height:(index + 1) * height, :] = panel[...]
    for step, amp in zip(steps, amps):
        at = pl.multiple_of((row ^ step) * pairs, pairs)
        lhs[pl.ds(at, pairs), :] = amp[...]


def assemble(steps, panels, amps):
    outs = [like(blocks[0], len(blocks) * blocks[0].shape[0], blocks[0].shape[1]) for blocks in (panels, amps)]
    args = [*panels, *amps]
    return call(functools.partial(assemble_kernel, steps), outs, [VMEM] * len(args), args)


def product(panels, lhs):
    return lax.dot_general(panels[...], lhs[...], (((1,), (1,)), ((), ())), preferred_element_type=jnp.float32)


def near_kernel(near, lhs, out):
    out[...] = product(near, lhs)


def contract_near(near, lhs):
    out = jax.ShapeDtypeStruct((near.shape[0], lhs.shape[0]), jnp.float32)
    return call(near_kernel, [out], [VMEM, VMEM], [near, lhs])[0]


def contract_kernel(steps, owner_ref, residual_ref, lhs, near_part, far, *refs):
    outs, ordered = refs[:-1], refs[-1]
    width = outs[0].shape[1]
    row, col = lax.axis_index("row"), lax.axis_index("col")
    columns = owner_ref.shape[1]
    height = ordered.shape[0] // columns
    per_row = width // height
    for half, part in enumerate((near_part[...], product(far, lhs))):
        for index in range(columns // 2):
            owner = owner_ref[0, col ^ (2 * index + half)]
            place = ((owner // per_row) ^ row) * per_row + owner % per_row
            at = pl.multiple_of(place * height, height)
            ordered[pl.ds(at, height), :] = part[index * height:(index + 1) * height, :]
    for step, out in zip(steps, outs):
        part = ordered[step * width:(step + 1) * width, :].T
        if step == 0:
            out[...] = part + residual_ref[...].reshape(part.shape)
        else:
            largest = jnp.max(jnp.abs(part), axis=0, keepdims=True)
            power = jnp.clip(14.0 - jnp.ceil(jnp.log2(jnp.maximum(largest, 1e-36))), -60.0, 120.0)
            out[:part.shape[0], :] = part * jnp.exp2(power)
            out[part.shape[0]:, :] = jnp.broadcast_to(power, (SCALE_ROWS, part.shape[1]))


def contract(steps, owner, residual, lhs, near_part, far):
    rows, ab = len(steps), 2 * far.shape[0]
    outs = [
        jax.ShapeDtypeStruct((lhs.shape[0] + (SCALE_ROWS if step else 0), ab // rows), jnp.float32) for step in steps]
    return call(
        functools.partial(contract_kernel, steps), outs, [SMEM] + [VMEM] * 4,
        [owner, residual, lhs, near_part, far], [pltpu.VMEM((ab, lhs.shape[0]), jnp.float32)],
    )


def exchange_partial(part, step):
    got = exchange(part.astype(jnp.float16), "row", step).astype(jnp.float32)
    return got[:-SCALE_ROWS] * jnp.exp2(-got[-SCALE_ROWS:1 - SCALE_ROWS])


def shards(amplitudes, integrals, panel_owner, residual_in):
    rows, columns = lax.axis_size("row"), lax.axis_size("col")
    steps = tuple(range(rows - 1, -1, -1))
    own, residual, owner, blocks = fetch(integrals, amplitudes, residual_in, panel_owner, rows)
    panels = [exchange(own, "col", step) if step else own for step in range(0, columns, 2)]
    amps = [exchange(blocks[step], "row", step) if step else blocks[0] for step in steps]
    near, lhs = assemble(steps, panels, amps)
    far = exchange(near, "col", 1)
    parts = contract(steps, owner, residual, lhs, contract_near(near, lhs), far)
    total = parts[-1]
    for step, part in zip(steps[-2::-1], parts[-2::-1]):
        total = total + exchange_partial(part, step)
    return total.reshape(residual_in.shape)


def solution(mesh):
    placed = (P("row", "col", None), P("col", "row"), P("row", None), P(None, "col", "row"))
    return jax.shard_map(
        shards, mesh=mesh, in_specs=placed, out_specs=P(None, "col", "row"), check_vma=False
    )
```

```python
import functools
import math

import jax
import jax.numpy as jnp
from jax import lax
from jax.experimental import pallas as pl
from jax.experimental.pallas import tpu as pltpu
from jax.sharding import PartitionSpec as P

VMEM = pl.BlockSpec(memory_space=pltpu.VMEM)
HBM = pl.BlockSpec(memory_space=pltpu.HBM)
SCALE_ROWS = 16
SWAPS = 2


def exchange(value, axis, step):
    n = lax.axis_size(axis)
    return lax.ppermute(value, axis, [(i, i ^ step) for i in range(n)])


def like(array, *shape):
    return jax.ShapeDtypeStruct(shape or array.shape, array.dtype)


def call(kernel, outs, specs, args, scratch=(), semaphores=()):
    size = sum(math.prod(x.shape) * jnp.dtype(x.dtype).itemsize for x in [*outs, *args, *scratch])
    return pl.pallas_call(
        kernel, out_shape=outs, in_specs=specs, out_specs=[VMEM] * len(outs), scratch_shapes=[*scratch, *semaphores],
        compiler_params=pltpu.CompilerParams(vmem_limit_bytes=size + (2 << 20)),
    )(*args)


def fetch_kernel(panel_ref, amp_ref, residual_ref, owner_ref, *refs):
    panel, residual, owner, blocks, sems = refs[0], refs[1], refs[2], refs[3:-1], refs[-1]
    width = blocks[0].shape[-1]
    row = lax.axis_index("row")
    pairs = [(panel_ref, panel), (residual_ref, residual), (owner_ref, owner)]
    for step, block in enumerate(blocks):
        at = pl.multiple_of((row ^ step) * width, width)
        pairs.append((amp_ref.at[0, :, pl.ds(at, width)], block))
    copies = [pltpu.make_async_copy(source, target, sems.at[i]) for i, (source, target) in enumerate(pairs)]
    for copy in copies:
        copy.start()
    for copy in copies:
        copy.wait()


def fetch(integrals, amplitudes, residual, owner, rows):
    _, pairs, kw = amplitudes.shape
    outs = [like(integrals), like(residual), like(owner)] + [like(amplitudes, pairs, kw // rows)] * rows
    args = [pltpu.with_memory_space_constraint(x, pltpu.HBM) for x in (integrals, amplitudes, residual, owner)]
    panel, residual, owner, *blocks = call(
        fetch_kernel, outs, [HBM] * 4, args, semaphores=[pltpu.SemaphoreType.DMA((len(outs),))])
    return panel, residual, owner, blocks


def assemble_kernel(steps, *refs):
    rows = len(steps)
    count = len(refs) - rows - SWAPS - 1
    panels, amps, nears, lhs = refs[:count], refs[count:count + rows], refs[count + rows:-1], refs[-1]
    height, pairs = panels[0].shape[0], amps[0].shape[0]
    row = lax.axis_index("row")
    for index, panel in enumerate(panels):
        near, place = nears[index * SWAPS // count], index % (count // SWAPS)
        near[place * height:(place + 1) * height, :] = panel[...]
    for step, amp in zip(steps, amps):
        at = pl.multiple_of((row ^ step) * pairs, pairs)
        lhs[pl.ds(at, pairs), :] = amp[...]


def assemble(steps, panels, amps):
    height, depth = panels[0].shape
    outs = [like(panels[0], len(panels) // SWAPS * height, depth)] * SWAPS
    outs.append(like(amps[0], len(amps) * amps[0].shape[0], depth))
    args = [*panels, *amps]
    *nears, lhs = call(functools.partial(assemble_kernel, steps), outs, [VMEM] * len(args), args)
    return nears, lhs


def product(panels, lhs):
    return lax.dot_general(panels[...], lhs[...], (((1,), (1,)), ((), ())), preferred_element_type=jnp.float32)


def product_kernel(lhs, *refs):
    panels, out = refs[:-1], refs[-1]
    height = panels[0].shape[0]
    for index, panel in enumerate(panels):
        out[index * height:(index + 1) * height, :] = product(panel, lhs)


def products(lhs, panels):
    out = jax.ShapeDtypeStruct((sum(panel.shape[0] for panel in panels), lhs.shape[0]), jnp.float32)
    return call(product_kernel, [out], [VMEM] * (1 + len(panels)), [lhs, *panels])[0]


def contract_kernel(steps, owner_ref, residual_ref, lhs, near_part, far_part, last, *refs):
    outs, ordered = refs[:-1], refs[-1]
    width = outs[0].shape[1]
    row, col = lax.axis_index("row"), lax.axis_index("col")
    owner = owner_ref[...]
    columns = owner.shape[1]
    height = ordered.shape[0] // columns
    per_row = width // height
    places = (((owner // per_row) ^ row) * per_row + owner % per_row).astype(jnp.float32)
    slots = lax.broadcasted_iota(jnp.int32, owner.shape, 1)
    blocks = [(near_part, 2 * index, index) for index in range(columns // 2)]
    blocks += [(far_part, 2 * index + 1, index) for index in range(far_part.shape[0] // height)]
    done = len(blocks) - columns // 2
    tail = product(last, lhs)
    blocks += [(tail, 2 * index + 1, index - done) for index in range(done, columns // 2)]
    for part, step, index in blocks:
        place = jnp.sum(jnp.where(slots == (col ^ step), places, 0.0)).astype(jnp.int32)
        at = pl.multiple_of(place * height, height)
        ordered[pl.ds(at, height), :] = part[index * height:(index + 1) * height, :]
    for step, out in zip(steps, outs):
        part = ordered[step * width:(step + 1) * width, :].T
        if step == 0:
            out[...] = part + residual_ref[...].reshape(part.shape)
        else:
            largest = jnp.max(jnp.abs(part), axis=0, keepdims=True)
            power = jnp.clip(14.0 - jnp.ceil(jnp.log2(jnp.maximum(largest, 1e-36))), -60.0, 120.0)
            out[:part.shape[0], :] = part * jnp.exp2(power)
            out[part.shape[0]:, :] = jnp.broadcast_to(power, (SCALE_ROWS, part.shape[1]))


def contract(steps, owner, residual, lhs, near_part, far_part, last):
    rows, ab = len(steps), 2 * near_part.shape[0]
    outs = [
        jax.ShapeDtypeStruct((lhs.shape[0] + (SCALE_ROWS if step else 0), ab // rows), jnp.float32) for step in steps]
    args = [owner, residual, lhs, near_part, far_part, last]
    return call(
        functools.partial(contract_kernel, steps), outs, [VMEM] * len(args), args,
        [pltpu.VMEM((ab, lhs.shape[0]), jnp.float32)],
    )


def exchange_partial(part, step):
    got = exchange(part.astype(jnp.float16), "row", step).astype(jnp.float32)
    return got[:-SCALE_ROWS] * jnp.exp2(-got[-SCALE_ROWS:1 - SCALE_ROWS])


def shards(amplitudes, integrals, panel_owner, residual_in):
    rows, columns = lax.axis_size("row"), lax.axis_size("col")
    steps = tuple(range(rows - 1, -1, -1))
    own, residual, owner, blocks = fetch(integrals, amplitudes, residual_in, panel_owner, rows)
    panels = [exchange(own, "col", step) if step else own for step in range(0, columns, 2)]
    amps = [exchange(blocks[step], "row", step) if step else blocks[0] for step in steps]
    nears, lhs = assemble(steps, panels, amps)
    *fars, last = [exchange(near, "col", 1) for near in nears]
    parts = contract(steps, owner, residual, lhs, products(lhs, nears), products(lhs, fars), last)
    total = parts[-1]
    for step, part in zip(steps[-2::-1], parts[-2::-1]):
        total = total + exchange_partial(part, step)
    return total.reshape(residual_in.shape)


def solution(mesh):
    placed = (P("row", "col", None), P("col", "row"), P("row", None), P(None, "col", "row"))
    return jax.shard_map(
        shards, mesh=mesh, in_specs=placed, out_specs=P(None, "col", "row"), check_vma=False
    )
```

```python
import functools
import math

import jax
import jax.numpy as jnp
from jax import lax
from jax.experimental import pallas as pl
from jax.experimental.pallas import tpu as pltpu
from jax.sharding import PartitionSpec as P

VMEM = pl.BlockSpec(memory_space=pltpu.VMEM)
HBM = pl.BlockSpec(memory_space=pltpu.HBM)
SCALE_ROWS = 16
SWAPS = 2


def exchange(value, axis, step):
    n = lax.axis_size(axis)
    return lax.ppermute(value, axis, [(i, i ^ step) for i in range(n)])


def like(array, *shape):
    return jax.ShapeDtypeStruct(shape or array.shape, array.dtype)


def call(kernel, outs, specs, args, scratch=(), semaphores=(), cost=None):
    size = sum(math.prod(x.shape) * jnp.dtype(x.dtype).itemsize for x in [*outs, *args, *scratch])
    return pl.pallas_call(
        kernel, out_shape=outs, in_specs=specs, out_specs=[VMEM] * len(outs), scratch_shapes=[*scratch, *semaphores],
        compiler_params=pltpu.CompilerParams(vmem_limit_bytes=size + (2 << 20)), cost_estimate=cost,
    )(*args)


def copy_all(pairs, sems):
    copies = [pltpu.make_async_copy(source, target, sems.at[i]) for i, (source, target) in enumerate(pairs)]
    for copy in copies:
        copy.start()
    for copy in copies:
        copy.wait()


def fetch_kernel(panel_ref, amp_ref, panel, *refs):
    blocks, sems = refs[:-1], refs[-1]
    width = blocks[0].shape[-1]
    row = lax.axis_index("row")
    pairs = [(panel_ref, panel)]
    for step, block in enumerate(blocks):
        at = pl.multiple_of((row ^ step) * width, width)
        pairs.append((amp_ref.at[0, :, pl.ds(at, width)], block))
    copy_all(pairs, sems)


def in_hbm(*arrays):
    return [pltpu.with_memory_space_constraint(x, pltpu.HBM) for x in arrays]


def fetch(integrals, amplitudes, rows):
    _, pairs, kw = amplitudes.shape
    outs = [like(integrals)] + [like(amplitudes, pairs, kw // rows)] * rows
    panel, *blocks = call(
        fetch_kernel, outs, [HBM] * 2, in_hbm(integrals, amplitudes), semaphores=[pltpu.SemaphoreType.DMA((len(outs),))])
    return panel, blocks


def fetch_late_kernel(residual_ref, owner_ref, residual, owner, sems):
    copy_all([(residual_ref, residual), (owner_ref, owner)], sems)


def fetch_late(residual, owner):
    cost = pl.CostEstimate(flops=0, bytes_accessed=16 << 20, transcendentals=0)
    return call(
        fetch_late_kernel, [like(residual), like(owner)], [HBM] * 2, in_hbm(residual, owner),
        semaphores=[pltpu.SemaphoreType.DMA((2,))], cost=cost)


def assemble_kernel(steps, residual_ref, owner_ref, *refs):
    rows, (residual, owner), refs = len(steps), refs[-2:], refs[:-2]
    residual[...] = residual_ref[...]
    owner[...] = owner_ref[...]
    count = len(refs) - rows - SWAPS - 1
    panels, amps, nears, lhs = refs[:count], refs[count:count + rows], refs[count + rows:-1], refs[-1]
    height, pairs = panels[0].shape[0], amps[0].shape[0]
    row = lax.axis_index("row")
    for index, panel in enumerate(panels):
        near, place = nears[index * SWAPS // count], index % (count // SWAPS)
        near[place * height:(place + 1) * height, :] = panel[...]
    for step, amp in zip(steps, amps):
        at = pl.multiple_of((row ^ step) * pairs, pairs)
        lhs[pl.ds(at, pairs), :] = amp[...]


def assemble(steps, residual, owner, panels, amps):
    height, depth = panels[0].shape
    outs = [like(panels[0], len(panels) // SWAPS * height, depth)] * SWAPS
    outs += [like(amps[0], len(amps) * amps[0].shape[0], depth), like(residual), like(owner)]
    args = [residual, owner, *panels, *amps]
    *nears, lhs, residual, owner = call(functools.partial(assemble_kernel, steps), outs, [VMEM] * len(args), args)
    return nears, lhs, residual, owner


def product(panels, lhs):
    return lax.dot_general(panels[...], lhs[...], (((1,), (1,)), ((), ())), preferred_element_type=jnp.float32)


def product_kernel(lhs, *refs):
    panels, out = refs[:-1], refs[-1]
    height = panels[0].shape[0]
    for index, panel in enumerate(panels):
        out[index * height:(index + 1) * height, :] = product(panel, lhs)


def products(lhs, panels):
    out = jax.ShapeDtypeStruct((sum(panel.shape[0] for panel in panels), lhs.shape[0]), jnp.float32)
    return call(product_kernel, [out], [VMEM] * (1 + len(panels)), [lhs, *panels])[0]


def contract_kernel(steps, owner_ref, residual_ref, lhs, near_part, far_part, last, *refs):
    outs, ordered = refs[:-1], refs[-1]
    width = outs[0].shape[1]
    row, col = lax.axis_index("row"), lax.axis_index("col")
    owner = owner_ref[...]
    columns = owner.shape[1]
    height = ordered.shape[0] // columns
    per_row = width // height
    places = (((owner // per_row) ^ row) * per_row + owner % per_row).astype(jnp.float32)
    slots = lax.broadcasted_iota(jnp.int32, owner.shape, 1)
    blocks = [(near_part, 2 * index, index) for index in range(columns // 2)]
    blocks += [(far_part, 2 * index + 1, index) for index in range(far_part.shape[0] // height)]
    done = len(blocks) - columns // 2
    tail = product(last, lhs)
    blocks += [(tail, 2 * index + 1, index - done) for index in range(done, columns // 2)]
    for part, step, index in blocks:
        place = jnp.sum(jnp.where(slots == (col ^ step), places, 0.0)).astype(jnp.int32)
        at = pl.multiple_of(place * height, height)
        ordered[pl.ds(at, height), :] = part[index * height:(index + 1) * height, :]
    for step, out in zip(steps, outs):
        part = ordered[step * width:(step + 1) * width, :].T
        if step == 0:
            out[...] = part + residual_ref[...].reshape(part.shape)
        else:
            largest = jnp.max(jnp.abs(part), axis=0, keepdims=True)
            power = jnp.clip(14.0 - jnp.ceil(jnp.log2(jnp.maximum(largest, 1e-36))), -60.0, 120.0)
            out[:part.shape[0], :] = part * jnp.exp2(power)
            out[part.shape[0]:, :] = jnp.broadcast_to(power, (SCALE_ROWS, part.shape[1]))


def contract(steps, owner, residual, lhs, near_part, far_part, last):
    rows, ab = len(steps), 2 * near_part.shape[0]
    outs = [
        jax.ShapeDtypeStruct((lhs.shape[0] + (SCALE_ROWS if step else 0), ab // rows), jnp.float32) for step in steps]
    args = [owner, residual, lhs, near_part, far_part, last]
    return call(
        functools.partial(contract_kernel, steps), outs, [VMEM] * len(args), args,
        [pltpu.VMEM((ab, lhs.shape[0]), jnp.float32)],
    )


def exchange_partial(part, step):
    got = exchange(part.astype(jnp.float16), "row", step).astype(jnp.float32)
    return got[:-SCALE_ROWS] * jnp.exp2(-got[-SCALE_ROWS:1 - SCALE_ROWS])


def shards(amplitudes, integrals, panel_owner, residual_in):
    rows, columns = lax.axis_size("row"), lax.axis_size("col")
    steps = tuple(range(rows - 1, -1, -1))
    own, blocks = fetch(integrals, amplitudes, rows)
    residual, owner = fetch_late(residual_in, panel_owner)
    panels = [exchange(own, "col", step) if step else own for step in range(0, columns, 2)]
    amps = [exchange(blocks[step], "row", step) if step else blocks[0] for step in steps]
    nears, lhs, residual, owner = assemble(steps, residual, owner, panels, amps)
    *fars, last = [exchange(near, "col", 1) for near in nears]
    parts = contract(steps, owner, residual, lhs, products(lhs, nears), products(lhs, fars), last)
    total = parts[-1]
    for step, part in zip(steps[-2::-1], parts[-2::-1]):
        total = total + exchange_partial(part, step)
    return total.reshape(residual_in.shape)


def solution(mesh):
    placed = (P("row", "col", None), P("col", "row"), P("row", None), P(None, "col", "row"))
    return jax.shard_map(
        shards, mesh=mesh, in_specs=placed, out_specs=P(None, "col", "row"), check_vma=False
    )
```

```python
import functools
import math

import jax
import jax.numpy as jnp
from jax import lax
from jax.experimental import pallas as pl
from jax.experimental.pallas import tpu as pltpu
from jax.sharding import PartitionSpec as P

VMEM = pl.BlockSpec(memory_space=pltpu.VMEM)
HBM = pl.BlockSpec(memory_space=pltpu.HBM)
SCALE_ROWS = 16
SWAPS = 2


def exchange(value, axis, step):
    n = lax.axis_size(axis)
    return lax.ppermute(value, axis, [(i, i ^ step) for i in range(n)])


def like(array, *shape):
    return jax.ShapeDtypeStruct(shape or array.shape, array.dtype)


def call(kernel, outs, specs, args, scratch=(), semaphores=(), cost=None):
    size = sum(math.prod(x.shape) * jnp.dtype(x.dtype).itemsize for x in [*outs, *args, *scratch])
    return pl.pallas_call(
        kernel, out_shape=outs, in_specs=specs, out_specs=[VMEM] * len(outs), scratch_shapes=[*scratch, *semaphores],
        compiler_params=pltpu.CompilerParams(vmem_limit_bytes=size + (2 << 20)), cost_estimate=cost,
    )(*args)


def copy_all(pairs, sems):
    copies = [pltpu.make_async_copy(source, target, sems.at[i]) for i, (source, target) in enumerate(pairs)]
    for copy in copies:
        copy.start()
    for copy in copies:
        copy.wait()


def fetch_kernel(panel_ref, amp_ref, panel, *refs):
    blocks, sems = refs[:-1], refs[-1]
    width = blocks[0].shape[-1]
    row = lax.axis_index("row")
    pairs = [(panel_ref, panel)]
    for step, block in enumerate(blocks):
        at = pl.multiple_of((row ^ step) * width, width)
        pairs.append((amp_ref.at[0, :, pl.ds(at, width)], block))
    copy_all(pairs, sems)


def in_hbm(*arrays):
    return [pltpu.with_memory_space_constraint(x, pltpu.HBM) for x in arrays]


def fetch(integrals, amplitudes, rows):
    _, pairs, kw = amplitudes.shape
    outs = [like(integrals)] + [like(amplitudes, pairs, kw // rows)] * rows
    panel, *blocks = call(
        fetch_kernel, outs, [HBM] * 2, in_hbm(integrals, amplitudes), semaphores=[pltpu.SemaphoreType.DMA((len(outs),))])
    return panel, blocks


def fetch_late_kernel(residual_ref, owner_ref, residual, owner, sems):
    copy_all([(residual_ref, residual), (owner_ref, owner)], sems)


def fetch_late(residual, owner):
    cost = pl.CostEstimate(flops=0, bytes_accessed=16 << 20, transcendentals=0)
    return call(
        fetch_late_kernel, [like(residual), like(owner)], [HBM] * 2, in_hbm(residual, owner),
        semaphores=[pltpu.SemaphoreType.DMA((2,))], cost=cost)


def assemble_kernel(steps, residual_ref, owner_ref, *refs):
    rows, (residual, owner), refs = len(steps), refs[-2:], refs[:-2]
    residual[...] = residual_ref[...]
    owner[...] = owner_ref[...]
    count = len(refs) - rows - SWAPS - 1
    panels, amps, nears, lhs = refs[:count], refs[count:count + rows], refs[count + rows:-1], refs[-1]
    height, pairs = panels[0].shape[0], amps[0].shape[0]
    row = lax.axis_index("row")
    for index, panel in enumerate(panels):
        near, place = nears[index * SWAPS // count], index % (count // SWAPS)
        near[place * height:(place + 1) * height, :] = panel[...]
    for step, amp in zip(steps, amps):
        at = pl.multiple_of((row ^ step) * pairs, pairs)
        lhs[pl.ds(at, pairs), :] = amp[...]


def assemble(steps, residual, owner, panels, amps):
    height, depth = panels[0].shape
    outs = [like(panels[0], len(panels) // SWAPS * height, depth)] * SWAPS
    outs += [like(amps[0], len(amps) * amps[0].shape[0], depth), like(residual), like(owner)]
    args = [residual, owner, *panels, *amps]
    *nears, lhs, residual, owner = call(functools.partial(assemble_kernel, steps), outs, [VMEM] * len(args), args)
    return nears, lhs, residual, owner


def product(panels, lhs):
    return lax.dot_general(panels[...], lhs[...], (((1,), (1,)), ((), ())), preferred_element_type=jnp.float32)


def product_kernel(lhs, *refs):
    panels, out = refs[:-1], refs[-1]
    height = panels[0].shape[0]
    for index, panel in enumerate(panels):
        out[index * height:(index + 1) * height, :] = product(panel, lhs)


def products(lhs, panels):
    out = jax.ShapeDtypeStruct((sum(panel.shape[0] for panel in panels), lhs.shape[0]), jnp.float32)
    return call(product_kernel, [out], [VMEM] * (1 + len(panels)), [lhs, *panels])[0]


def contract_kernel(steps, owner_ref, residual_ref, lhs, near_part, far_part, last, *refs):
    outs, ordered = refs[:-1], refs[-1]
    width = outs[0].shape[1]
    row, col = lax.axis_index("row"), lax.axis_index("col")
    owner = owner_ref[...]
    columns = owner.shape[1]
    height = ordered.shape[0] // columns
    per_row = width // height
    places = (((owner // per_row) ^ row) * per_row + owner % per_row).astype(jnp.float32)
    slots = lax.broadcasted_iota(jnp.int32, owner.shape, 1)
    blocks = [(near_part, 2 * index, index) for index in range(columns // 2)]
    blocks += [(far_part, 2 * index + 1, index) for index in range(far_part.shape[0] // height)]
    done = len(blocks) - columns // 2
    tail = product(last, lhs)
    blocks += [(tail, 2 * index + 1, index - done) for index in range(done, columns // 2)]
    for part, step, index in blocks:
        place = jnp.sum(jnp.where(slots == (col ^ step), places, 0.0)).astype(jnp.int32)
        at = pl.multiple_of(place * height, height)
        ordered[pl.ds(at, height), :] = part[index * height:(index + 1) * height, :]
    for step, out in zip(steps, outs):
        part = ordered[step * width:(step + 1) * width, :].T
        if step == 0:
            out[...] = part + residual_ref[...].reshape(part.shape)
        else:
            largest = jnp.max(jnp.abs(part), axis=0, keepdims=True)
            power = jnp.clip(14.0 - jnp.ceil(jnp.log2(jnp.maximum(largest, 1e-36))), -60.0, 120.0)
            out[:part.shape[0], :] = part * jnp.exp2(power)
            out[part.shape[0]:, :] = jnp.broadcast_to(power, (SCALE_ROWS, part.shape[1]))


def contract(steps, owner, residual, lhs, near_part, far_part, last):
    rows, ab = len(steps), 2 * near_part.shape[0]
    outs = [
        jax.ShapeDtypeStruct((lhs.shape[0] + (SCALE_ROWS if step else 0), ab // rows), jnp.float32) for step in steps]
    args = [owner, residual, lhs, near_part, far_part, last]
    return call(
        functools.partial(contract_kernel, steps), outs, [VMEM] * len(args), args,
        [pltpu.VMEM((ab, lhs.shape[0]), jnp.float32)],
    )


def exchange_partial(part, step):
    got = exchange(part.astype(jnp.float16), "row", step)
    power = got[-SCALE_ROWS:1 - SCALE_ROWS].astype(jnp.float32)
    return got[:-SCALE_ROWS].astype(jnp.float32) * jnp.exp2(-power)


def shards(amplitudes, integrals, panel_owner, residual_in):
    rows, columns = lax.axis_size("row"), lax.axis_size("col")
    steps = tuple(range(rows - 1, -1, -1))
    own, blocks = fetch(integrals, amplitudes, rows)
    residual, owner = fetch_late(residual_in, panel_owner)
    panels = [exchange(own, "col", step) if step else own for step in range(0, columns, 2)]
    amps = [exchange(blocks[step], "row", step) if step else blocks[0] for step in steps]
    nears, lhs, residual, owner = assemble(steps, residual, owner, panels, amps)
    *fars, last = [exchange(near, "col", 1) for near in nears]
    parts = contract(steps, owner, residual, lhs, products(lhs, nears), products(lhs, fars), last)
    total = parts[-1]
    for step, part in zip(steps[-2::-1], parts[-2::-1]):
        total = total + exchange_partial(part, step)
    return total.reshape(residual_in.shape)


def solution(mesh):
    placed = (P("row", "col", None), P("col", "row"), P("row", None), P(None, "col", "row"))
    return jax.shard_map(
        shards, mesh=mesh, in_specs=placed, out_specs=P(None, "col", "row"), check_vma=False
    )
```

```python
import functools
import math

import jax
import jax.numpy as jnp
from jax import lax
from jax.experimental import pallas as pl
from jax.experimental.pallas import tpu as pltpu
from jax.sharding import PartitionSpec as P

VMEM = pl.BlockSpec(memory_space=pltpu.VMEM)
HBM = pl.BlockSpec(memory_space=pltpu.HBM)
SCALE_ROWS = 16
SWAPS = 2


def exchange(value, axis, step):
    n = lax.axis_size(axis)
    return lax.ppermute(value, axis, [(i, i ^ step) for i in range(n)])


def like(array, *shape):
    return jax.ShapeDtypeStruct(shape or array.shape, array.dtype)


def call(kernel, outs, specs, args, scratch=(), semaphores=(), cost=None):
    size = sum(math.prod(x.shape) * jnp.dtype(x.dtype).itemsize for x in [*outs, *args, *scratch])
    return pl.pallas_call(
        kernel, out_shape=outs, in_specs=specs, out_specs=[VMEM] * len(outs), scratch_shapes=[*scratch, *semaphores],
        compiler_params=pltpu.CompilerParams(vmem_limit_bytes=size + (2 << 20)), cost_estimate=cost,
    )(*args)


def copy_all(pairs, sems):
    copies = [pltpu.make_async_copy(source, target, sems.at[i]) for i, (source, target) in enumerate(pairs)]
    for copy in copies:
        copy.start()
    for copy in copies:
        copy.wait()


def fetch_kernel(panel_ref, amp_ref, panel, *refs):
    blocks, sems = refs[:-1], refs[-1]
    width = blocks[0].shape[-1]
    row = lax.axis_index("row")
    pairs = [(panel_ref, panel)]
    for step, block in enumerate(blocks):
        at = pl.multiple_of((row ^ step) * width, width)
        pairs.append((amp_ref.at[0, :, pl.ds(at, width)], block))
    copy_all(pairs, sems)


def in_hbm(*arrays):
    return [pltpu.with_memory_space_constraint(x, pltpu.HBM) for x in arrays]


def fetch(integrals, amplitudes, rows):
    _, pairs, kw = amplitudes.shape
    outs = [like(integrals)] + [like(amplitudes, pairs, kw // rows)] * rows
    panel, *blocks = call(
        fetch_kernel, outs, [HBM] * 2, in_hbm(integrals, amplitudes), semaphores=[pltpu.SemaphoreType.DMA((len(outs),))])
    return panel, blocks


def fetch_late_kernel(residual_ref, owner_ref, residual, owner, sems):
    copy_all([(residual_ref, residual), (owner_ref, owner)], sems)


def fetch_late(residual, owner):
    cost = pl.CostEstimate(flops=0, bytes_accessed=256 << 20, transcendentals=0)
    return call(
        fetch_late_kernel, [like(residual), like(owner)], [HBM] * 2, in_hbm(residual, owner),
        semaphores=[pltpu.SemaphoreType.DMA((2,))], cost=cost)


def assemble_kernel(steps, residual_ref, owner_ref, *refs):
    rows, (residual, owner), refs = len(steps), refs[-2:], refs[:-2]
    residual[...] = residual_ref[...]
    owner[...] = owner_ref[...]
    count = len(refs) - rows - SWAPS - 1
    panels, amps, nears, lhs = refs[:count], refs[count:count + rows], refs[count + rows:-1], refs[-1]
    height, pairs = panels[0].shape[0], amps[0].shape[0]
    row = lax.axis_index("row")
    for index, panel in enumerate(panels):
        near, place = nears[index * SWAPS // count], index % (count // SWAPS)
        near[place * height:(place + 1) * height, :] = panel[...]
    for step, amp in zip(steps, amps):
        at = pl.multiple_of((row ^ step) * pairs, pairs)
        lhs[pl.ds(at, pairs), :] = amp[...]


def assemble(steps, residual, owner, panels, amps):
    height, depth = panels[0].shape
    outs = [like(panels[0], len(panels) // SWAPS * height, depth)] * SWAPS
    outs += [like(amps[0], len(amps) * amps[0].shape[0], depth), like(residual), like(owner)]
    args = [residual, owner, *panels, *amps]
    *nears, lhs, residual, owner = call(functools.partial(assemble_kernel, steps), outs, [VMEM] * len(args), args)
    return nears, lhs, residual, owner


def product(panels, lhs):
    return lax.dot_general(panels[...], lhs[...], (((1,), (1,)), ((), ())), preferred_element_type=jnp.float32)


def product_kernel(lhs, *refs):
    panels, out = refs[:-1], refs[-1]
    height = panels[0].shape[0]
    for index, panel in enumerate(panels):
        out[index * height:(index + 1) * height, :] = product(panel, lhs)


def products(lhs, panels):
    out = jax.ShapeDtypeStruct((sum(panel.shape[0] for panel in panels), lhs.shape[0]), jnp.float32)
    return call(product_kernel, [out], [VMEM] * (1 + len(panels)), [lhs, *panels])[0]


def contract_kernel(steps, owner_ref, residual_ref, lhs, near_part, far_part, last, *refs):
    outs, ordered = refs[:-1], refs[-1]
    width = outs[0].shape[1]
    row, col = lax.axis_index("row"), lax.axis_index("col")
    owner = owner_ref[...]
    columns = owner.shape[1]
    height = ordered.shape[0] // columns
    per_row = width // height
    places = (((owner // per_row) ^ row) * per_row + owner % per_row).astype(jnp.float32)
    slots = lax.broadcasted_iota(jnp.int32, owner.shape, 1)
    blocks = [(near_part, 2 * index, index) for index in range(columns // 2)]
    blocks += [(far_part, 2 * index + 1, index) for index in range(far_part.shape[0] // height)]
    done = len(blocks) - columns // 2
    tail = product(last, lhs)
    blocks += [(tail, 2 * index + 1, index - done) for index in range(done, columns // 2)]
    for part, step, index in blocks:
        place = jnp.sum(jnp.where(slots == (col ^ step), places, 0.0)).astype(jnp.int32)
        at = pl.multiple_of(place * height, height)
        ordered[pl.ds(at, height), :] = part[index * height:(index + 1) * height, :]
    for step, out in zip(steps, outs):
        part = ordered[step * width:(step + 1) * width, :].T
        if step == 0:
            out[...] = part + residual_ref[...].reshape(part.shape)
        else:
            largest = jnp.max(jnp.abs(part), axis=0, keepdims=True)
            power = jnp.clip(14.0 - jnp.ceil(jnp.log2(jnp.maximum(largest, 1e-36))), -60.0, 120.0)
            out[:part.shape[0], :] = part * jnp.exp2(power)
            out[part.shape[0]:, :] = jnp.broadcast_to(power, (SCALE_ROWS, part.shape[1]))


def contract(steps, owner, residual, lhs, near_part, far_part, last):
    rows, ab = len(steps), 2 * near_part.shape[0]
    outs = [
        jax.ShapeDtypeStruct((lhs.shape[0] + (SCALE_ROWS if step else 0), ab // rows), jnp.float32) for step in steps]
    args = [owner, residual, lhs, near_part, far_part, last]
    return call(
        functools.partial(contract_kernel, steps), outs, [VMEM] * len(args), args,
        [pltpu.VMEM((ab, lhs.shape[0]), jnp.float32)],
    )


def exchange_partial(part, step):
    got = exchange(part.astype(jnp.float16), "row", step).astype(jnp.float32)
    return got[:-SCALE_ROWS] * jnp.exp2(-got[-SCALE_ROWS:1 - SCALE_ROWS])


def shards(amplitudes, integrals, panel_owner, residual_in):
    rows, columns = lax.axis_size("row"), lax.axis_size("col")
    steps = tuple(range(rows - 1, -1, -1))
    own, blocks = fetch(integrals, amplitudes, rows)
    residual, owner = fetch_late(residual_in, panel_owner)
    panels = [exchange(own, "col", step) if step else own for step in range(0, columns, 2)]
    amps = [exchange(blocks[step], "row", step) if step else blocks[0] for step in steps]
    nears, lhs, residual, owner = assemble(steps, residual, owner, panels, amps)
    *fars, last = [exchange(near, "col", 1) for near in nears]
    parts = contract(steps, owner, residual, lhs, products(lhs, nears), products(lhs, fars), last)
    total = parts[-1]
    for step, part in zip(steps[-2::-1], parts[-2::-1]):
        total = total + exchange_partial(part, step)
    return total.reshape(residual_in.shape)


def solution(mesh):
    placed = (P("row", "col", None), P("col", "row"), P("row", None), P(None, "col", "row"))
    return jax.shard_map(
        shards, mesh=mesh, in_specs=placed, out_specs=P(None, "col", "row"), check_vma=False
    )
```

```python
import functools
import math

import jax
import jax.numpy as jnp
from jax import lax
from jax.experimental import pallas as pl
from jax.experimental.pallas import tpu as pltpu
from jax.sharding import PartitionSpec as P

VMEM = pl.BlockSpec(memory_space=pltpu.VMEM)
HBM = pl.BlockSpec(memory_space=pltpu.HBM)
SCALE_ROWS = 16
SWAPS = 2


def exchange(value, axis, step):
    n = lax.axis_size(axis)
    return lax.ppermute(value, axis, [(i, i ^ step) for i in range(n)])


def like(array, *shape):
    return jax.ShapeDtypeStruct(shape or array.shape, array.dtype)


def call(kernel, outs, specs, args, scratch=(), semaphores=(), cost=None):
    size = sum(math.prod(x.shape) * jnp.dtype(x.dtype).itemsize for x in [*outs, *args, *scratch])
    return pl.pallas_call(
        kernel, out_shape=outs, in_specs=specs, out_specs=[VMEM] * len(outs), scratch_shapes=[*scratch, *semaphores],
        compiler_params=pltpu.CompilerParams(vmem_limit_bytes=size + (2 << 20)), cost_estimate=cost,
    )(*args)


def copy_all(pairs, sems):
    copies = [pltpu.make_async_copy(source, target, sems.at[i]) for i, (source, target) in enumerate(pairs)]
    for copy in copies:
        copy.start()
    for copy in copies:
        copy.wait()


def fetch_kernel(panel_ref, amp_ref, panel, *refs):
    blocks, sems = refs[:-1], refs[-1]
    width = blocks[0].shape[-1]
    row = lax.axis_index("row")
    pairs = [(panel_ref, panel)]
    for step, block in enumerate(blocks):
        at = pl.multiple_of((row ^ step) * width, width)
        pairs.append((amp_ref.at[0, :, pl.ds(at, width)], block))
    copy_all(pairs, sems)


def in_hbm(*arrays):
    return [pltpu.with_memory_space_constraint(x, pltpu.HBM) for x in arrays]


def fetch(integrals, amplitudes, rows):
    _, pairs, kw = amplitudes.shape
    outs = [like(integrals)] + [like(amplitudes, pairs, kw // rows)] * rows
    panel, *blocks = call(
        fetch_kernel, outs, [HBM] * 2, in_hbm(integrals, amplitudes), semaphores=[pltpu.SemaphoreType.DMA((len(outs),))])
    return panel, blocks


def fetch_late_kernel(residual_ref, owner_ref, residual, owner, sems):
    copy_all([(residual_ref, residual), (owner_ref, owner)], sems)


def fetch_late(residual, owner):
    cost = pl.CostEstimate(flops=0, bytes_accessed=16 << 20, transcendentals=0)
    return call(
        fetch_late_kernel, [like(residual), like(owner)], [HBM] * 2, in_hbm(residual, owner),
        semaphores=[pltpu.SemaphoreType.DMA((2,))], cost=cost)


def assemble_kernel(steps, residual_ref, owner_ref, *refs):
    rows, (residual, owner), refs = len(steps), refs[-2:], refs[:-2]
    residual[...] = residual_ref[...]
    owner[...] = owner_ref[...]
    count = len(refs) - rows - SWAPS - 1
    panels, amps, nears, lhs = refs[:count], refs[count:count + rows], refs[count + rows:-1], refs[-1]
    height, pairs = panels[0].shape[0], amps[0].shape[0]
    row = lax.axis_index("row")
    for index, panel in enumerate(panels):
        near, place = nears[index * SWAPS // count], index % (count // SWAPS)
        near[place * height:(place + 1) * height, :] = panel[...]
    for step, amp in zip(steps, amps):
        at = pl.multiple_of((row ^ step) * pairs, pairs)
        lhs[pl.ds(at, pairs), :] = amp[...]


def assemble(steps, residual, owner, panels, amps):
    height, depth = panels[0].shape
    outs = [like(panels[0], len(panels) // SWAPS * height, depth)] * SWAPS
    outs += [like(amps[0], len(amps) * amps[0].shape[0], depth), like(residual), like(owner)]
    args = [residual, owner, *panels, *amps]
    *nears, lhs, residual, owner = call(functools.partial(assemble_kernel, steps), outs, [VMEM] * len(args), args)
    return nears, lhs, residual, owner


def product(panels, lhs):
    return lax.dot_general(panels[...], lhs[...], (((1,), (1,)), ((), ())), preferred_element_type=jnp.float32)


def product_kernel(lhs, *refs):
    panels, out = refs[:-1], refs[-1]
    height = panels[0].shape[0]
    for index, panel in enumerate(panels):
        out[index * height:(index + 1) * height, :] = product(panel, lhs)


def products(lhs, panels):
    out = jax.ShapeDtypeStruct((sum(panel.shape[0] for panel in panels), lhs.shape[0]), jnp.float32)
    return call(product_kernel, [out], [VMEM] * (1 + len(panels)), [lhs, *panels])[0]


def contract_kernel(steps, owner_ref, residual_ref, lhs, near_part, far_part, last, *refs):
    outs, ordered = refs[:-1], refs[-1]
    width = outs[0].shape[1]
    row, col = lax.axis_index("row"), lax.axis_index("col")
    owner = owner_ref[...]
    columns = owner.shape[1]
    height = ordered.shape[0] // columns
    per_row = width // height
    places = (((owner // per_row) ^ row) * per_row + owner % per_row).astype(jnp.float32)
    slots = lax.broadcasted_iota(jnp.int32, owner.shape, 1)
    blocks = [(near_part, 2 * index, index) for index in range(columns // 2)]
    blocks += [(far_part, 2 * index + 1, index) for index in range(far_part.shape[0] // height)]
    done = len(blocks) - columns // 2
    tail = product(last, lhs)
    blocks += [(tail, 2 * index + 1, index - done) for index in range(done, columns // 2)]
    for part, step, index in blocks:
        place = jnp.sum(jnp.where(slots == (col ^ step), places, 0.0)).astype(jnp.int32)
        at = pl.multiple_of(place * height, height)
        ordered[pl.ds(at, height), :] = part[index * height:(index + 1) * height, :]
    for step, out in zip(steps, outs):
        part = ordered[step * width:(step + 1) * width, :].T
        if step == 0:
            out[...] = part + residual_ref[...].reshape(part.shape)
        else:
            largest = jnp.max(jnp.abs(part), axis=0, keepdims=True)
            power = jnp.clip(14.0 - jnp.ceil(jnp.log2(jnp.maximum(largest, 1e-36))), -60.0, 120.0)
            out[:part.shape[0], :] = part * jnp.exp2(power)
            out[part.shape[0]:, :] = jnp.broadcast_to(power, (SCALE_ROWS, part.shape[1]))


def contract(steps, owner, residual, lhs, near_part, far_part, last):
    rows, ab = len(steps), 2 * near_part.shape[0]
    outs = [
        jax.ShapeDtypeStruct((lhs.shape[0] + (SCALE_ROWS if step else 0), ab // rows), jnp.float32) for step in steps]
    args = [owner, residual, lhs, near_part, far_part, last]
    return call(
        functools.partial(contract_kernel, steps), outs, [VMEM] * len(args), args,
        [pltpu.VMEM((ab, lhs.shape[0]), jnp.float32)],
    )


def exchange_partial(part, step):
    got = exchange(part.astype(jnp.float16), "row", step).astype(jnp.float32)
    return got[:-SCALE_ROWS] * jnp.exp2(-got[-SCALE_ROWS:1 - SCALE_ROWS])


def shards(amplitudes, integrals, panel_owner, residual_in):
    rows, columns = lax.axis_size("row"), lax.axis_size("col")
    steps = tuple(range(rows - 1, -1, -1))
    own, blocks = fetch(integrals, amplitudes, rows)
    residual, owner = fetch_late(residual_in, panel_owner)
    panels = [exchange(own, "col", step) if step else own for step in range(0, columns, 2)]
    order = (rows // 2, *(step for step in steps if step != rows // 2))
    amps = [exchange(blocks[step], "row", step) if step else blocks[0] for step in order]
    nears, lhs, residual, owner = assemble(order, residual, owner, panels, amps)
    *fars, last = [exchange(near, "col", 1) for near in nears]
    parts = contract(steps, owner, residual, lhs, products(lhs, nears), products(lhs, fars), last)
    total = parts[-1]
    for step, part in zip(steps[-2::-1], parts[-2::-1]):
        total = total + exchange_partial(part, step)
    return total.reshape(residual_in.shape)


def solution(mesh):
    placed = (P("row", "col", None), P("col", "row"), P("row", None), P(None, "col", "row"))
    return jax.shard_map(
        shards, mesh=mesh, in_specs=placed, out_specs=P(None, "col", "row"), check_vma=False
    )
```

```python
import functools
import math

import jax
import jax.numpy as jnp
from jax import lax
from jax.experimental import pallas as pl
from jax.experimental.pallas import tpu as pltpu
from jax.sharding import PartitionSpec as P

VMEM = pl.BlockSpec(memory_space=pltpu.VMEM)
HBM = pl.BlockSpec(memory_space=pltpu.HBM)
SCALE_ROWS = 16
SWAPS = 2


def exchange(value, axis, step):
    n = lax.axis_size(axis)
    return lax.ppermute(value, axis, [(i, i ^ step) for i in range(n)])


def like(array, *shape):
    return jax.ShapeDtypeStruct(shape or array.shape, array.dtype)


def call(kernel, outs, specs, args, scratch=(), semaphores=(), cost=None):
    size = sum(math.prod(x.shape) * jnp.dtype(x.dtype).itemsize for x in [*outs, *args, *scratch])
    return pl.pallas_call(
        kernel, out_shape=outs, in_specs=specs, out_specs=[VMEM] * len(outs), scratch_shapes=[*scratch, *semaphores],
        compiler_params=pltpu.CompilerParams(vmem_limit_bytes=size + (2 << 20)), cost_estimate=cost,
    )(*args)


def copy_all(pairs, sems):
    copies = [pltpu.make_async_copy(source, target, sems.at[i]) for i, (source, target) in enumerate(pairs)]
    for copy in copies:
        copy.start()
    for copy in copies:
        copy.wait()


def fetch_kernel(panel_ref, amp_ref, panel, *refs):
    blocks, sems = refs[:-1], refs[-1]
    width = blocks[0].shape[-1]
    row = lax.axis_index("row")
    pairs = [(panel_ref, panel)]
    for step, block in enumerate(blocks):
        at = pl.multiple_of((row ^ step) * width, width)
        pairs.append((amp_ref.at[0, :, pl.ds(at, width)], block))
    copy_all(pairs, sems)


def in_hbm(*arrays):
    return [pltpu.with_memory_space_constraint(x, pltpu.HBM) for x in arrays]


def fetch(integrals, amplitudes, rows):
    _, pairs, kw = amplitudes.shape
    outs = [like(integrals)] + [like(amplitudes, pairs, kw // rows)] * rows
    panel, *blocks = call(
        fetch_kernel, outs, [HBM] * 2, in_hbm(integrals, amplitudes), semaphores=[pltpu.SemaphoreType.DMA((len(outs),))])
    return panel, blocks


def fetch_late_kernel(residual_ref, owner_ref, residual, owner, sems):
    copy_all([(residual_ref, residual), (owner_ref, owner)], sems)


def fetch_late(residual, owner):
    cost = pl.CostEstimate(flops=0, bytes_accessed=16 << 20, transcendentals=0)
    return call(
        fetch_late_kernel, [like(residual), like(owner)], [HBM] * 2, in_hbm(residual, owner),
        semaphores=[pltpu.SemaphoreType.DMA((2,))], cost=cost)


def assemble_kernel(steps, residual_ref, owner_ref, *refs):
    rows, (residual, owner), refs = len(steps), refs[-2:], refs[:-2]
    residual[...] = residual_ref[...]
    owner[...] = owner_ref[...]
    count = len(refs) - rows - SWAPS - 1
    panels, amps, nears, lhs = refs[:count], refs[count:count + rows], refs[count + rows:-1], refs[-1]
    height, pairs = panels[0].shape[0], amps[0].shape[0]
    row = lax.axis_index("row")
    for index, panel in enumerate(panels):
        near, place = nears[index * SWAPS // count], index % (count // SWAPS)
        near[place * height:(place + 1) * height, :] = panel[...]
    for step, amp in zip(steps, amps):
        at = pl.multiple_of((row ^ step) * pairs, pairs)
        lhs[pl.ds(at, pairs), :] = amp[...]


def assemble(steps, residual, owner, panels, amps):
    height, depth = panels[0].shape
    outs = [like(panels[0], len(panels) // SWAPS * height, depth)] * SWAPS
    outs += [like(amps[0], len(amps) * amps[0].shape[0], depth), like(residual), like(owner)]
    args = [residual, owner, *panels, *amps]
    *nears, lhs, residual, owner = call(functools.partial(assemble_kernel, steps), outs, [VMEM] * len(args), args)
    return nears, lhs, residual, owner


def product(panels, lhs):
    return lax.dot_general(panels[...], lhs[...], (((1,), (1,)), ((), ())), preferred_element_type=jnp.float32)


def product_kernel(lhs, *refs):
    panels, out = refs[:-1], refs[-1]
    height = panels[0].shape[0]
    for index, panel in enumerate(panels):
        out[index * height:(index + 1) * height, :] = product(panel, lhs)


def products(lhs, panels):
    out = jax.ShapeDtypeStruct((sum(panel.shape[0] for panel in panels), lhs.shape[0]), jnp.float32)
    return call(product_kernel, [out], [VMEM] * (1 + len(panels)), [lhs, *panels])[0]


def contract_kernel(steps, owner_ref, residual_ref, lhs, near_part, far_part, last, *refs):
    outs, ordered = refs[:-1], refs[-1]
    width = outs[0].shape[1]
    row, col = lax.axis_index("row"), lax.axis_index("col")
    owner = owner_ref[...]
    columns = owner.shape[1]
    height = ordered.shape[0] // columns
    per_row = width // height
    places = (((owner // per_row) ^ row) * per_row + owner % per_row).astype(jnp.float32)
    slots = lax.broadcasted_iota(jnp.int32, owner.shape, 1)
    blocks = [(near_part, 2 * index, index) for index in range(columns // 2)]
    blocks += [(far_part, 2 * index + 1, index) for index in range(far_part.shape[0] // height)]
    done = len(blocks) - columns // 2
    tail = product(last, lhs)
    blocks += [(tail, 2 * index + 1, index - done) for index in range(done, columns // 2)]
    for part, step, index in blocks:
        place = jnp.sum(jnp.where(slots == (col ^ step), places, 0.0)).astype(jnp.int32)
        at = pl.multiple_of(place * height, height)
        ordered[pl.ds(at, height), :] = part[index * height:(index + 1) * height, :]
    for step, out in zip(steps, outs):
        part = ordered[step * width:(step + 1) * width, :].T
        if step == 0:
            out[...] = part + residual_ref[...].reshape(part.shape)
        else:
            largest = jnp.max(jnp.abs(part), axis=0, keepdims=True)
            power = jnp.clip(14.0 - jnp.ceil(jnp.log2(jnp.maximum(largest, 1e-36))), -60.0, 120.0)
            out[:part.shape[0], :] = part * jnp.exp2(power)
            out[part.shape[0]:, :] = jnp.broadcast_to(power, (SCALE_ROWS, part.shape[1]))


def contract(steps, owner, residual, lhs, near_part, far_part, last):
    rows, ab = len(steps), 2 * near_part.shape[0]
    outs = [
        jax.ShapeDtypeStruct((lhs.shape[0] + (SCALE_ROWS if step else 0), ab // rows), jnp.float32) for step in steps]
    args = [owner, residual, lhs, near_part, far_part, last]
    return call(
        functools.partial(contract_kernel, steps), outs, [VMEM] * len(args), args,
        [pltpu.VMEM((ab, lhs.shape[0]), jnp.float32)],
    )


def exchange_partial(part, step):
    got = exchange(part.astype(jnp.float16), "row", step).astype(jnp.float32)
    return got[:-SCALE_ROWS] * jnp.exp2(-got[-SCALE_ROWS:1 - SCALE_ROWS])


def shards(amplitudes, integrals, panel_owner, residual_in):
    rows, columns = lax.axis_size("row"), lax.axis_size("col")
    steps = tuple(range(rows - 1, -1, -1))
    own, blocks = fetch(integrals, amplitudes, rows)
    residual, owner = fetch_late(residual_in, panel_owner)
    panels = [exchange(own, "col", step) if step else own for step in range(0, columns, 2)]
    amps = [exchange(blocks[step], "row", step) if step else blocks[0] for step in steps]
    nears, lhs, residual, owner = assemble(steps, residual, owner, panels, amps)
    *fars, last = [exchange(near, "col", 1) for near in nears]
    parts = contract(steps, owner, residual, lhs, products(lhs, nears), products(lhs, fars), last)
    total = parts[-1]
    middle_last = sorted(range(1, rows), key=lambda step: (step == rows // 2, step))
    for step in middle_last:
        total = total + exchange_partial(parts[steps.index(step)], step)
    return total.reshape(residual_in.shape)


def solution(mesh):
    placed = (P("row", "col", None), P("col", "row"), P("row", None), P(None, "col", "row"))
    return jax.shard_map(
        shards, mesh=mesh, in_specs=placed, out_specs=P(None, "col", "row"), check_vma=False
    )
```
